32 devices in a mesh: replica: 8 (over y, x, core), fsdp: 4 (over z).
Axes of the slice: x: 2, y: 2, z: 4, core: 2. Of those that a mesh axis runs over, the one named last changes fastest.
Arguments:
- hidden_one: bfloat16 [8192, 7168], P(('replica', 'fsdp')), may hold values from -6 to 6
- hidden_two: bfloat16 [8192, 7168], P(('replica', 'fsdp')), may hold values from -6 to 6
- targets_one: bfloat16 [8192, 512], P(('replica', 'fsdp')), may hold values from -6 to 6
- targets_two: bfloat16 [8192, 512], P(('replica', 'fsdp')), may hold values from -6 to 6
- value_weight: bfloat16 [8, 7168, 512], P('replica', 'fsdp'), may hold values from -6 to 6
- fragment: int32 [1], replicated, may hold values from 0 to 4095
- outer_params: float32 [4, 32, 7168], P(None, 'fsdp'), may hold values from -6 to 6
- outer_momentum: float32 [4, 32, 7168], P(None, 'fsdp'), may hold values from -6 to 6
- local_params: bfloat16 [8, 4, 32, 7168], P('replica', None, 'fsdp'), may hold values from -12 to 12
Outputs:
- new_weight: bfloat16 [8, 7168, 512], P('replica', 'fsdp')
- errors_two: bfloat16 [8192, 512], P(('replica', 'fsdp'))
- merged_params: float32 [32, 7168], P('fsdp')
- merged_momentum: float32 [32, 7168], P('fsdp')
The draws below stay inside these ranges and needn't reach their ends.
All inputs are finite; a program needn't handle non-finite values.
Results may differ from the reference program's by a relative error of at most 0.009.
Values may be sent and summed in bfloat16 or wider, within the bound.
A program may use at most 128 MiB of HBM per device.

```python
import jax
import jax.numpy as jnp
from jax import lax

D = 7168
K = 512
TOK_DEV = 256
FRAGS = 4
FROWS = 32
REPLICAS = 8
TOKENS = 8192
N_REPLICA = 8
N_FSDP = 4


def common_params(key):
    return jnp.clip(jax.random.normal(key, (FRAGS, FROWS, D), jnp.float32), -6.0, 6.0)


def draw_outer_params(key, part):
    return common_params(key)


def draw_local_params(key, part):
    base = common_params(key)
    key = jax.random.fold_in(key, 7)
    first = jax.random.fold_in(key, 0)
    shape = (REPLICAS, FRAGS, FROWS, D)
    ramp = 0.2 + 0.4 * jnp.arange(REPLICAS, dtype=jnp.float32) / max(REPLICAS - 1, 1)
    drift = jnp.clip(jax.random.normal(first, shape, jnp.float32), -6.0, 6.0)
    return (base[None] + ramp[:, None, None, None] * drift).astype(jnp.bfloat16)


def block_scale(rng, extent, pieces, smallest, high):
    gain, own = 1.0, jax.random.fold_in(rng, 6)
    for position, shards_of in pieces:
        steps = jnp.exp(jax.random.uniform(jax.random.fold_in(own, position), (shards_of,), jnp.float32, smallest / len(pieces), high / len(pieces)))
        gain = gain * jnp.repeat(steps, extent[position] // shards_of).reshape([-1 if axis == position else 1 for axis in range(len(extent))])
    return gain


def bell_draw(own_key, dims, scale, reach, cuts=(), kind=jnp.bfloat16):
    values = scale * jax.random.normal(own_key, dims, jnp.float32)
    if cuts:
        values = values * block_scale(own_key, dims, cuts, -0.22, 0.18)
    return jnp.clip(values, -reach, reach).astype(kind)


def setup_inputs(seed: int = 0) -> dict:
    seeds = jax.random.split(jax.random.key(seed), 10)
    return {
        "hidden_one": bell_draw(seeds[0], (TOKENS, D), 1.0, 6.0, ((0, 32),)),
        "hidden_two": bell_draw(seeds[1], (TOKENS, D), 1.0, 6.0, ((0, 32),)),
        "targets_one": bell_draw(seeds[2], (TOKENS, K), 1.0, 6.0, ((0, 32),)),
        "targets_two": bell_draw(seeds[3], (TOKENS, K), 1.0, 6.0, ((0, 32),)),
        "value_weight": bell_draw(seeds[4], (REPLICAS, D, K), 1.0, 6.0, ((0, 8), (1, 4))),
        "fragment": jax.random.randint(seeds[5], (1,), 0, 4096).astype(jnp.int32),
        "outer_params": draw_outer_params(jax.random.fold_in(seeds[9], 71), 0),
        "outer_momentum": bell_draw(seeds[7], (FRAGS, FROWS, D), 0.5, 6.0, ((1, 4),), jnp.float32),
        "local_params": draw_local_params(jax.random.fold_in(seeds[9], 71), 0),
    }


EPS = 1e-06
LEARN_RATE = 0.3
OUTER_RATE = 0.7
MOMENTUM = 0.9

def normalize(rows):
    wide = rows.astype(jnp.float32)
    scale = lax.rsqrt(lax.optimization_barrier(jnp.mean(wide * wide, axis=1, keepdims=True)) + EPS)
    return (wide * scale).astype(jnp.bfloat16)

def gradient(normed, errors, factor):
    parts = normed.reshape(N_FSDP, TOK_DEV, D)
    errs = errors.reshape(N_FSDP, TOK_DEV, K)

    def add_block(carry, pair):
        term = lax.dot_general(pair[0], pair[1], (((0,), (0,)), ((), ())), preferred_element_type=jnp.float32) * factor
        rounded = lax.optimization_barrier(term.astype(jnp.bfloat16))
        return (carry + rounded.astype(jnp.float32), None)
    total, unused = lax.scan(add_block, jnp.zeros((D, K), jnp.float32), (parts, errs))
    return total

def replica_step(inputs):
    first, second, aim_one, aim_two, weight = inputs
    factor = D ** (-0.5)
    normed_one = normalize(first)
    normed_two = normalize(second)
    values_one = jnp.dot(normed_one, weight, preferred_element_type=jnp.float32) * factor
    errors_one = (values_one - aim_one.astype(jnp.float32)).astype(jnp.bfloat16)
    weight_next = (weight.astype(jnp.float32) - LEARN_RATE * gradient(normed_one, errors_one, factor)).astype(jnp.bfloat16)
    values_two = jnp.dot(normed_two, weight_next, preferred_element_type=jnp.float32) * factor
    errors_two = (values_two - aim_two.astype(jnp.float32)).astype(jnp.bfloat16)
    weight_last = (weight_next.astype(jnp.float32) - LEARN_RATE * gradient(normed_two, errors_two, factor)).astype(jnp.bfloat16)
    return (weight_last, errors_two)

def reference(hidden_one, hidden_two, targets_one, targets_two, value_weight, fragment, outer_params, outer_momentum, local_params):
    per_replica = N_FSDP * TOK_DEV
    new_weight, errors_two = lax.map(replica_step, (hidden_one.reshape(N_REPLICA, per_replica, D), hidden_two.reshape(N_REPLICA, per_replica, D), targets_one.reshape(N_REPLICA, per_replica, K), targets_two.reshape(N_REPLICA, per_replica, K), value_weight))
    errors_two = errors_two.reshape(N_REPLICA * per_replica, K)
    chosen = (fragment[0] % FRAGS).astype(jnp.int32)
    params_now = lax.dynamic_index_in_dim(outer_params, chosen, 0, keepdims=False)
    moment_now = lax.dynamic_index_in_dim(outer_momentum, chosen, 0, keepdims=False)
    local_now = lax.dynamic_index_in_dim(local_params, chosen, 1, keepdims=False)
    terms = lax.optimization_barrier((params_now[None] - local_now.astype(jnp.float32)).astype(jnp.bfloat16))
    outer_grad = lax.optimization_barrier(jnp.sum(terms.astype(jnp.float32), axis=0)) / N_REPLICA
    merged_momentum = MOMENTUM * moment_now + outer_grad
    merged_params = params_now - OUTER_RATE * (outer_grad + MOMENTUM * merged_momentum)
    return (new_weight, errors_two, merged_params, merged_momentum)
```

```python
import jax
import jax.numpy as jnp
from jax import lax
from jax.sharding import PartitionSpec as P

EPS = 1e-06
LEARN_RATE = 0.3
OUTER_RATE = 0.7
MOMENTUM = 0.9


def normalize(rows):
    wide = rows.astype(jnp.float32)
    scale = lax.rsqrt(jnp.mean(wide * wide, axis=1, keepdims=True) + EPS)
    return (wide * scale).astype(jnp.bfloat16)


def row_sums(columns, shard, factor):
    part = jnp.dot(columns, shard, preferred_element_type=jnp.float32) * factor
    pieces = lax.all_to_all(
        part.astype(jnp.bfloat16), "fsdp", split_axis=0, concat_axis=0, tiled=True
    )
    pieces = pieces.reshape(lax.axis_size("fsdp"), -1, part.shape[1])
    return jnp.sum(pieces.astype(jnp.float32), axis=0)


def block_gradient(columns_all, errors_all, blocks, factor):
    tokens = columns_all.shape[0] // blocks
    parts = columns_all.reshape(blocks, tokens, columns_all.shape[1])
    errs = errors_all.reshape(blocks, tokens, errors_all.shape[1])
    terms = (
        lax.dot_general(
            parts, errs, (((0, 1), (0, 1)), ((), ())), preferred_element_type=jnp.float32
        )
        * factor
    )
    return terms


def per_device(
    hidden_one,
    hidden_two,
    targets_one,
    targets_two,
    value_weight,
    fragment,
    outer_params,
    outer_momentum,
    local_params,
):
    width = hidden_one.shape[1]
    factor = width ** (-0.5)
    blocks = lax.axis_size("fsdp")
    normed_one = normalize(hidden_one)
    normed_two = normalize(hidden_two)
    weight_shard = value_weight[0]
    cols_one = lax.all_to_all(normed_one, "fsdp", split_axis=1, concat_axis=0, tiled=True)
    cols_two = lax.all_to_all(normed_two, "fsdp", split_axis=1, concat_axis=0, tiled=True)
    values_one = row_sums(cols_one, weight_shard, factor)
    errors_one = (values_one - targets_one.astype(jnp.float32)).astype(jnp.bfloat16)
    errs_one = lax.all_gather(errors_one, "fsdp", axis=0, tiled=True)
    grad_one = block_gradient(cols_one, errs_one, blocks, factor)
    next_shard = (weight_shard.astype(jnp.float32) - LEARN_RATE * grad_one).astype(jnp.bfloat16)
    values_two = row_sums(cols_two, next_shard, factor)
    errors_two = (values_two - targets_two.astype(jnp.float32)).astype(jnp.bfloat16)
    errs_two = lax.all_gather(errors_two, "fsdp", axis=0, tiled=True)
    grad_two = block_gradient(cols_two, errs_two, blocks, factor)
    new_shard = (next_shard.astype(jnp.float32) - LEARN_RATE * grad_two).astype(jnp.bfloat16)
    chosen = fragment[0] % outer_params.shape[0]
    params_now = lax.dynamic_index_in_dim(outer_params, chosen, 0, keepdims=False)
    moment_now = lax.dynamic_index_in_dim(outer_momentum, chosen, 0, keepdims=False)
    local_now = lax.dynamic_index_in_dim(local_params[0], chosen, 0, keepdims=False)
    outer_term = params_now - local_now.astype(jnp.float32)
    replicas = lax.axis_size("replica")
    outer_grad = lax.psum(outer_term.astype(jnp.bfloat16), "replica").astype(jnp.float32) / replicas
    merged_momentum = MOMENTUM * moment_now + outer_grad
    merged_params = params_now - OUTER_RATE * (outer_grad + MOMENTUM * merged_momentum)
    return (new_shard[None], errors_two, merged_params, merged_momentum)


def solution(mesh):
    return jax.shard_map(
        per_device,
        mesh=mesh,
        in_specs=(
            P(("replica", "fsdp"), None),
            P(("replica", "fsdp"), None),
            P(("replica", "fsdp"), None),
            P(("replica", "fsdp"), None),
            P("replica", "fsdp", None),
            P(),
            P(None, "fsdp", None),
            P(None, "fsdp", None),
            P("replica", None, "fsdp", None),
        ),
        out_specs=(
            P("replica", "fsdp", None),
            P(("replica", "fsdp"), None),
            P("fsdp", None),
            P("fsdp", None),
        ),
        check_vma=False,
    )
```

```python
import functools

import jax
import jax.numpy as jnp
from jax import lax
from jax.experimental import pallas as pl
from jax.experimental.pallas import tpu as pltpu
from jax.sharding import PartitionSpec as P

EPS = 1e-06
LEARN_RATE = 0.3
OUTER_RATE = 0.7
MOMENTUM = 0.9
MESH = pl.DeviceIdType.MESH
PIECES = 4
WINDOW = 2


def tile_of(extent):
    return 256 if extent % 256 == 0 else 128


def steps_kernel(
    n,
    h_one,
    h_two,
    t_one,
    t_two,
    w_ref,
    out_w,
    out_e,
    hv,
    xs,
    w_next,
    grad,
    scale,
    vs,
    ra,
    mine,
    rb_out,
    rb_in,
    errs,
    l_sem,
    x_send,
    x_recv,
    a_send,
    a_recv,
    b_send,
    b_recv,
    c_send,
    c_recv,
    i_send,
    i_recv,
    f_send,
    f_recv,
):
    tokens, width = h_one.shape
    cols, feats = w_ref.shape
    tp = tokens // PIECES
    half = n // 2
    factor = width ** (-0.5)
    me = lax.axis_index("fsdp")
    side, spot = me // half, me % half
    other = 1 - side
    cross = other * half + spot
    hidden = (h_one, h_two)
    targets = (t_one, t_two)

    barrier = pltpu.get_barrier_semaphore()
    for d in range(1, n):
        pl.semaphore_signal(
            barrier, inc=1, device_id={"fsdp": lax.rem(me + d, n)}, device_id_type=MESH
        )
    pl.semaphore_wait(barrier, n - 1)

    def remote(src, dst, send, recv, peer):
        return pltpu.make_async_remote_copy(
            src_ref=src,
            dst_ref=dst,
            send_sem=send,
            recv_sem=recv,
            device_id={"fsdp": peer},
            device_id_type=MESH,
        )

    def rows_of(block):
        return pl.ds(pl.multiple_of(block * tp, tp), tp)

    def cols_of(block):
        return pl.ds(pl.multiple_of(block * cols, 128), cols)

    def x_copies(k):
        s, p = k // PIECES, k % PIECES
        out = []
        for d in range(1, n):
            peer = lax.rem(me + d, n)
            out.append(
                remote(
                    hidden[s].at[pl.ds(p * tp, tp), cols_of(peer)],
                    xs.at[s, p, rows_of(me), :],
                    x_send.at[s, p, d - 1],
                    x_recv.at[s, p, d - 1],
                    peer,
                )
            )
        return out

    def half_peers():
        return [(d - 1, side * half + lax.rem(spot + d, half)) for d in range(1, half)]

    def a_copies(s, p):
        return [
            remote(
                vs.at[s, p, :, rows_of(peer - side * half), :],
                ra.at[s, p, d],
                a_send.at[s, p, d],
                a_recv.at[s, p, d],
                peer,
            )
            for d, peer in half_peers()
        ]

    def b_copy(s, p):
        return remote(
            rb_out.at[s, p], rb_in.at[s, p], b_send.at[s, p], b_recv.at[s, p], cross
        )

    def c_copy(s, p):
        piece = errs.at[s, p, rows_of(me), :]
        return remote(piece, piece, c_send.at[s, p], c_recv.at[s, p], cross)

    def i_copies(s, p):
        piece = errs.at[s, p, rows_of(me), :]
        return [
            remote(piece, piece, i_send.at[s, p, d], i_recv.at[s, p, d], peer)
            for d, peer in half_peers()
        ]

    def f_copies(s, p):
        piece = errs.at[s, p, rows_of(cross), :]
        return [
            remote(piece, piece, f_send.at[s, p, d], f_recv.at[s, p, d], peer)
            for d, peer in half_peers()
        ]

    issued = [0]

    def pump():
        k = issued[0]
        if k == 2 * PIECES:
            return
        if k >= WINDOW:
            for copy in x_copies(k - WINDOW):
                copy.wait_send()
        for copy in x_copies(k):
            copy.start()
        issued[0] = k + 1

    for _ in range(WINDOW):
        pump()
    loads = []
    for s in range(2):
        loads.append(pltpu.make_async_copy(hidden[s], hv.at[s], l_sem.at[s, PIECES]))
        for p in range(PIECES):
            loads.append(
                pltpu.make_async_copy(
                    hidden[s].at[pl.ds(p * tp, tp), cols_of(me)],
                    xs.at[s, p, rows_of(me), :],
                    l_sem.at[s, p],
                )
            )
    for copy in loads:
        copy.start()
    for copy in loads:
        copy.wait()
    for s in range(2):

        @pl.loop(0, tokens // 16)
        def _(i):
            rows = pl.ds(pl.multiple_of(i * 16, 16), 16)
            wide = hv[s, rows, :].astype(jnp.float32)
            mean = jnp.sum(wide * wide, axis=1, keepdims=True) * (1.0 / width)
            scale[s, rows, :] = jnp.broadcast_to(lax.rsqrt(mean + EPS), (16, 128))

    def stage_a(s, p):
        weight = w_ref if s == 0 else w_next
        for copy in x_copies(s * PIECES + p):
            copy.wait_recv()
        pump()
        nt = tile_of(feats)

        @pl.loop(0, feats // nt)
        def _(j):
            lanes = pl.ds(pl.multiple_of(j * nt, nt), nt)
            part = jnp.dot(xs[s, p], weight[:, lanes], preferred_element_type=jnp.float32)
            vs[s, p, :, :, lanes] = part.astype(jnp.bfloat16).reshape(2, half * tp, nt)

        for copy in a_copies(s, p):
            copy.start()

    def stage_b(s, p):
        copies = a_copies(s, p)
        for copy in copies:
            copy.wait_recv()
        spots = rows_of(spot)
        away = vs[s, p, other, spots, :].astype(jnp.float32)
        here = vs[s, p, side, spots, :].astype(jnp.float32)
        for d in range(half - 1):
            away = away + ra[s, p, d, other].astype(jnp.float32)
            here = here + ra[s, p, d, side].astype(jnp.float32)
        rb_out[s, p] = away.astype(jnp.bfloat16)
        b_copy(s, p).start()
        mine[s, p] = here

    def stage_c(s, p):
        b_copy(s, p).wait_recv()
        rows = pl.ds(p * tp, tp)
        gain = scale[s, rows, :][:, :1]
        total = mine[s, p] + rb_in[s, p].astype(jnp.float32)
        err = total * (gain * factor) - targets[s][rows, :].astype(jnp.float32)
        err = err.astype(jnp.bfloat16)
        if s == 1:
            out_e[rows, :] = err
        errs[s, p, rows_of(me), :] = (err.astype(jnp.float32) * gain).astype(jnp.bfloat16)
        c_copy(s, p).start()
        for copy in i_copies(s, p):
            copy.start()

    def stage_d(s, p):
        c_copy(s, p).wait_recv()
        for copy in f_copies(s, p):
            copy.start()

    ct = tile_of(cols)

    def stage_f(s, p):
        for copy in i_copies(s, p) + f_copies(s, p):
            copy.wait_recv()
        source = w_ref if s == 0 else w_next
        target = w_next if s == 0 else out_w

        @pl.loop(0, cols // ct)
        def _(j):
            lanes = pl.ds(pl.multiple_of(j * ct, ct), ct)
            term = lax.dot_general(
                xs[s, p, :, lanes],
                errs[s, p],
                (((0,), (0,)), ((), ())),
                preferred_element_type=jnp.float32,
            )
            if p > 0:
                term = grad[lanes, :] + term
            if p < PIECES - 1:
                grad[lanes, :] = term
            else:
                old = source[lanes, :].astype(jnp.float32)
                target[lanes, :] = (old - (LEARN_RATE * factor) * term).astype(jnp.bfloat16)

    stages = (stage_a, stage_b, stage_c, stage_d, stage_f)
    depth = len(stages)
    for s in range(2):
        for t in range(PIECES + depth - 1):
            for lag in range(depth - 1, -1, -1):
                if 0 <= t - lag < PIECES:
                    stages[lag](s, t - lag)
            if t >= PIECES:
                pump()

    for k in range(2 * PIECES - WINDOW, 2 * PIECES):
        for copy in x_copies(k):
            copy.wait_send()
    for s in range(2):
        for p in range(PIECES):
            for copy in a_copies(s, p) + i_copies(s, p) + f_copies(s, p):
                copy.wait_send()
            b_copy(s, p).wait_send()
            c_copy(s, p).wait_send()


def two_steps(hidden_one, hidden_two, targets_one, targets_two, weight):
    n = lax.axis_size("fsdp")
    half = n // 2
    tokens, width = hidden_one.shape
    cols, feats = weight.shape
    tp = tokens // PIECES
    bf, f32 = jnp.bfloat16, jnp.float32
    anywhere = pl.BlockSpec(memory_space=pl.ANY)
    vmem = pl.BlockSpec(memory_space=pltpu.VMEM)
    pair = pltpu.SemaphoreType.DMA((2, PIECES))
    peers = pltpu.SemaphoreType.DMA((2, PIECES, half - 1))
    others = pltpu.SemaphoreType.DMA((2, PIECES, n - 1))
    return pl.pallas_call(
        functools.partial(steps_kernel, n),
        out_shape=(
            jax.ShapeDtypeStruct((cols, feats), bf),
            jax.ShapeDtypeStruct((tokens, feats), bf),
        ),
        in_specs=[anywhere, anywhere, vmem, vmem, vmem],
        out_specs=(vmem, vmem),
        scratch_shapes=[
            pltpu.VMEM((2, tokens, width), bf),
            pltpu.VMEM((2, PIECES, n * tp, cols), bf),
            pltpu.VMEM((cols, feats), bf),
            pltpu.VMEM((cols, feats), f32),
            pltpu.VMEM((2, tokens, 128), f32),
            pltpu.VMEM((2, PIECES, 2, half * tp, feats), bf),
            pltpu.VMEM((2, PIECES, half - 1, 2, tp, feats), bf),
            pltpu.VMEM((2, PIECES, tp, feats), f32),
            pltpu.VMEM((2, PIECES, tp, feats), bf),
            pltpu.VMEM((2, PIECES, tp, feats), bf),
            pltpu.VMEM((2, PIECES, n * tp, feats), bf),
            pltpu.SemaphoreType.DMA((2, PIECES + 1)),
            others,
            others,
            peers,
            peers,
            pair,
            pair,
            pair,
            pair,
            peers,
            peers,
            peers,
            peers,
        ],
        compiler_params=pltpu.CompilerParams(
            collective_id=0, has_side_effects=True, vmem_limit_bytes=56 * 1024 * 1024
        ),
        cost_estimate=pl.CostEstimate(
            flops=8 * n * tokens * cols * feats,
            bytes_accessed=200 * 1024 * 1024,
            transcendentals=0,
        ),
    )(hidden_one, hidden_two, targets_one, targets_two, weight)


def per_device(
    hidden_one,
    hidden_two,
    targets_one,
    targets_two,
    value_weight,
    fragment,
    outer_params,
    outer_momentum,
    local_params,
):
    chosen = fragment[0] % outer_params.shape[0]
    params_now = lax.dynamic_index_in_dim(outer_params, chosen, 0, keepdims=False)
    moment_now = lax.dynamic_index_in_dim(outer_momentum, chosen, 0, keepdims=False)
    local_now = lax.dynamic_index_in_dim(local_params[0], chosen, 0, keepdims=False)
    outer_term = params_now - local_now.astype(jnp.float32)
    replicas = lax.axis_size("replica")
    outer_grad = lax.psum(outer_term.astype(jnp.bfloat16), "replica").astype(jnp.float32) / replicas
    merged_momentum = MOMENTUM * moment_now + outer_grad
    merged_params = params_now - OUTER_RATE * (outer_grad + MOMENTUM * merged_momentum)
    new_shard, errors_two = two_steps(
        hidden_one, hidden_two, targets_one, targets_two, value_weight[0]
    )
    return (new_shard[None], errors_two, merged_params, merged_momentum)


def solution(mesh):
    return jax.shard_map(
        per_device,
        mesh=mesh,
        in_specs=(
            P(("replica", "fsdp"), None),
            P(("replica", "fsdp"), None),
            P(("replica", "fsdp"), None),
            P(("replica", "fsdp"), None),
            P("replica", "fsdp", None),
            P(),
            P(None, "fsdp", None),
            P(None, "fsdp", None),
            P("replica", None, "fsdp", None),
        ),
        out_specs=(
            P("replica", "fsdp", None),
            P(("replica", "fsdp"), None),
            P("fsdp", None),
            P("fsdp", None),
        ),
        check_vma=False,
    )
```

```python
import functools

import jax
import jax.numpy as jnp
from jax import lax
from jax.experimental import pallas as pl
from jax.experimental.pallas import tpu as pltpu
from jax.sharding import PartitionSpec as P

EPS = 1e-06
LEARN_RATE = 0.3
OUTER_RATE = 0.7
MOMENTUM = 0.9
MESH = pl.DeviceIdType.MESH
PIECES = 4
WINDOW = 2


def tile_of(extent):
    return 256 if extent % 256 == 0 else 128


def steps_kernel(
    n,
    replicas,
    h_one,
    h_two,
    t_one_hbm,
    t_two_hbm,
    w_hbm,
    fragment,
    params_hbm,
    momentum_hbm,
    local_hbm,
    out_w,
    out_e,
    out_params,
    out_momentum,
    t_one,
    t_two,
    w_ref,
    params,
    momentum,
    local,
    outer_sum,
    outer_in,
    hv,
    xs,
    w_next,
    grad,
    scale,
    vs,
    ra,
    mine,
    rb_out,
    rb_in,
    errs,
    l_sem,
    x_send,
    x_recv,
    a_send,
    a_recv,
    b_send,
    b_recv,
    c_send,
    c_recv,
    i_send,
    i_recv,
    f_send,
    f_recv,
    o_load,
    o_send,
    o_recv,
):
    tokens, width = h_one.shape
    cols, feats = w_ref.shape
    tp = tokens // PIECES
    half = n // 2
    factor = width ** (-0.5)
    me = lax.axis_index("fsdp")
    side, spot = me // half, me % half
    other = 1 - side
    cross = other * half + spot
    hidden = (h_one, h_two)
    targets = (t_one, t_two)

    mine_r = lax.axis_index("replica")
    levels = replicas.bit_length() - 1
    outer_peers = []
    for k in range(levels):
        step = 2**k
        outer_peers.append(mine_r + (1 - 2 * ((mine_r // step) % 2)) * step)

    barrier = pltpu.get_barrier_semaphore()
    for d in range(1, n):
        pl.semaphore_signal(
            barrier, inc=1, device_id={"fsdp": lax.rem(me + d, n)}, device_id_type=MESH
        )
    for peer in outer_peers:
        pl.semaphore_signal(barrier, inc=1, device_id={"replica": peer}, device_id_type=MESH)
    pl.semaphore_wait(barrier, n - 1 + len(outer_peers))

    def remote(src, dst, send, recv, peer):
        return pltpu.make_async_remote_copy(
            src_ref=src,
            dst_ref=dst,
            send_sem=send,
            recv_sem=recv,
            device_id={"fsdp": peer},
            device_id_type=MESH,
        )

    def rows_of(block):
        return pl.ds(pl.multiple_of(block * tp, tp), tp)

    def cols_of(block):
        return pl.ds(pl.multiple_of(block * cols, 128), cols)

    def x_copies(k):
        s, p = k // PIECES, k % PIECES
        out = []
        for d in range(1, n):
            peer = lax.rem(me + d, n)
            out.append(
                remote(
                    hidden[s].at[pl.ds(p * tp, tp), cols_of(peer)],
                    xs.at[s, p, rows_of(me), :],
                    x_send.at[s, p, d - 1],
                    x_recv.at[s, p, d - 1],
                    peer,
                )
            )
        return out

    def half_peers():
        return [(d - 1, side * half + lax.rem(spot + d, half)) for d in range(1, half)]

    def a_copies(s, p):
        return [
            remote(
                vs.at[s, p, :, rows_of(peer - side * half), :],
                ra.at[s, p, d],
                a_send.at[s, p, d],
                a_recv.at[s, p, d],
                peer,
            )
            for d, peer in half_peers()
        ]

    def b_copy(s, p):
        return remote(
            rb_out.at[s, p], rb_in.at[s, p], b_send.at[s, p], b_recv.at[s, p], cross
        )

    def c_copy(s, p):
        piece = errs.at[s, p, rows_of(me), :]
        return remote(piece, piece, c_send.at[s, p], c_recv.at[s, p], cross)

    def i_copies(s, p):
        piece = errs.at[s, p, rows_of(me), :]
        return [
            remote(piece, piece, i_send.at[s, p, d], i_recv.at[s, p, d], peer)
            for d, peer in half_peers()
        ]

    def f_copies(s, p):
        piece = errs.at[s, p, rows_of(cross), :]
        return [
            remote(piece, piece, f_send.at[s, p, d], f_recv.at[s, p, d], peer)
            for d, peer in half_peers()
        ]

    issued = [0]

    def pump():
        k = issued[0]
        if k == 2 * PIECES:
            return
        if k >= WINDOW:
            for copy in x_copies(k - WINDOW):
                copy.wait_send()
        for copy in x_copies(k):
            copy.start()
        issued[0] = k + 1

    for _ in range(WINDOW):
        pump()
    loads = []
    for s in range(2):
        loads.append(pltpu.make_async_copy(hidden[s], hv.at[s], l_sem.at[s, PIECES]))
        for p in range(PIECES):
            loads.append(
                pltpu.make_async_copy(
                    hidden[s].at[pl.ds(p * tp, tp), cols_of(me)],
                    xs.at[s, p, rows_of(me), :],
                    l_sem.at[s, p],
                )
            )
    outer_loads = []
    for i, (src, dst) in enumerate(
        (
            (params_hbm, params),
            (local_hbm, local),
            (momentum_hbm, momentum),
            (w_hbm, w_ref),
            (t_one_hbm, t_one),
            (t_two_hbm, t_two),
        )
    ):
        outer_loads.append(pltpu.make_async_copy(src, dst, o_load.at[i]))
    for copy in outer_loads + loads:
        copy.start()
    for copy in outer_loads:
        copy.wait()
    chosen = lax.rem(fragment[0], params_hbm.shape[0])

    def outer_copy(k):
        return pltpu.make_async_remote_copy(
            src_ref=outer_sum.at[k],
            dst_ref=outer_in.at[k],
            send_sem=o_send.at[k],
            recv_sem=o_recv.at[k],
            device_id={"replica": outer_peers[k]},
            device_id_type=MESH,
        )

    term = params[chosen] - local[chosen].astype(jnp.float32)
    outer_sum[0] = term.astype(jnp.bfloat16).astype(jnp.float32)
    outer_copy(0).start()
    for copy in loads:
        copy.wait()
    for s in range(2):

        @pl.loop(0, tokens // 16)
        def _(i):
            rows = pl.ds(pl.multiple_of(i * 16, 16), 16)
            wide = hv[s, rows, :].astype(jnp.float32)
            mean = jnp.sum(wide * wide, axis=1, keepdims=True) * (1.0 / width)
            scale[s, rows, :] = jnp.broadcast_to(lax.rsqrt(mean + EPS), (16, 128))

    def outer_level(k):
        outer_copy(k).wait_recv()
        total = outer_sum[k] + outer_in[k]
        if k + 1 < levels:
            outer_sum[k + 1] = total
            outer_copy(k + 1).start()
            return
        outer_grad = total * (1.0 / replicas)
        merged = MOMENTUM * momentum[chosen] + outer_grad
        out_momentum[...] = merged
        out_params[...] = params[chosen] - OUTER_RATE * (outer_grad + MOMENTUM * merged)

    outer_done = [0]

    def stage_a(s, p):
        weight = w_ref if s == 0 else w_next
        for copy in x_copies(s * PIECES + p):
            copy.wait_recv()
        pump()
        nt = tile_of(feats)

        @pl.loop(0, feats // nt)
        def _(j):
            lanes = pl.ds(pl.multiple_of(j * nt, nt), nt)
            part = jnp.dot(xs[s, p], weight[:, lanes], preferred_element_type=jnp.float32)
            vs[s, p, :, :, lanes] = part.astype(jnp.bfloat16).reshape(2, half * tp, nt)

        for copy in a_copies(s, p):
            copy.start()

    def stage_b(s, p):
        copies = a_copies(s, p)
        for copy in copies:
            copy.wait_recv()
        spots = rows_of(spot)
        away = vs[s, p, other, spots, :].astype(jnp.float32)
        here = vs[s, p, side, spots, :].astype(jnp.float32)
        for d in range(half - 1):
            away = away + ra[s, p, d, other].astype(jnp.float32)
            here = here + ra[s, p, d, side].astype(jnp.float32)
        rb_out[s, p] = away.astype(jnp.bfloat16)
        b_copy(s, p).start()
        mine[s, p] = here

    def stage_c(s, p):
        b_copy(s, p).wait_recv()
        rows = pl.ds(p * tp, tp)
        gain = scale[s, rows, :][:, :1]
        total = mine[s, p] + rb_in[s, p].astype(jnp.float32)
        err = total * (gain * factor) - targets[s][rows, :].astype(jnp.float32)
        err = err.astype(jnp.bfloat16)
        if s == 1:
            out_e[rows, :] = err
        errs[s, p, rows_of(me), :] = (err.astype(jnp.float32) * gain).astype(jnp.bfloat16)
        c_copy(s, p).start()
        for copy in i_copies(s, p):
            copy.start()

    def stage_d(s, p):
        c_copy(s, p).wait_recv()
        for copy in f_copies(s, p):
            copy.start()

    ct = tile_of(cols)

    def stage_f(s, p):
        for copy in i_copies(s, p) + f_copies(s, p):
            copy.wait_recv()
        source = w_ref if s == 0 else w_next
        target = w_next if s == 0 else out_w

        @pl.loop(0, cols // ct)
        def _(j):
            lanes = pl.ds(pl.multiple_of(j * ct, ct), ct)
            term = lax.dot_general(
                xs[s, p, :, lanes],
                errs[s, p],
                (((0,), (0,)), ((), ())),
                preferred_element_type=jnp.float32,
            )
            if p > 0:
                term = grad[lanes, :] + term
            if p < PIECES - 1:
                grad[lanes, :] = term
            else:
                old = source[lanes, :].astype(jnp.float32)
                target[lanes, :] = (old - (LEARN_RATE * factor) * term).astype(jnp.bfloat16)

    stages = (stage_a, stage_b, stage_c, stage_d, stage_f)
    depth = len(stages)
    for s in range(2):
        for t in range(PIECES + depth - 1):
            for lag in range(depth - 1, -1, -1):
                if 0 <= t - lag < PIECES:
                    stages[lag](s, t - lag)
            if t >= PIECES:
                pump()
            if outer_done[0] < levels:
                outer_level(outer_done[0])
                outer_done[0] += 1

    for k in range(levels):
        outer_copy(k).wait_send()
    for k in range(2 * PIECES - WINDOW, 2 * PIECES):
        for copy in x_copies(k):
            copy.wait_send()
    for s in range(2):
        for p in range(PIECES):
            for copy in a_copies(s, p) + i_copies(s, p) + f_copies(s, p):
                copy.wait_send()
            b_copy(s, p).wait_send()
            c_copy(s, p).wait_send()


def per_device(
    hidden_one,
    hidden_two,
    targets_one,
    targets_two,
    value_weight,
    fragment,
    outer_params,
    outer_momentum,
    local_params,
):
    weight = value_weight[0]
    n = lax.axis_size("fsdp")
    replicas = lax.axis_size("replica")
    levels = replicas.bit_length() - 1
    frows = outer_params.shape[1]
    half = n // 2
    tokens, width = hidden_one.shape
    cols, feats = weight.shape
    tp = tokens // PIECES
    bf, f32 = jnp.bfloat16, jnp.float32
    anywhere = pl.BlockSpec(memory_space=pl.ANY)
    vmem = pl.BlockSpec(memory_space=pltpu.VMEM)
    pair = pltpu.SemaphoreType.DMA((2, PIECES))
    peers = pltpu.SemaphoreType.DMA((2, PIECES, half - 1))
    others = pltpu.SemaphoreType.DMA((2, PIECES, n - 1))
    new_shard, errors_two, merged_params, merged_momentum = pl.pallas_call(
        functools.partial(steps_kernel, n, replicas),
        out_shape=(
            jax.ShapeDtypeStruct((cols, feats), bf),
            jax.ShapeDtypeStruct((tokens, feats), bf),
            jax.ShapeDtypeStruct((frows, width), f32),
            jax.ShapeDtypeStruct((frows, width), f32),
        ),
        in_specs=[anywhere] * 5 + [pl.BlockSpec(memory_space=pltpu.SMEM)] + [anywhere] * 3,
        out_specs=(vmem, vmem, vmem, vmem),
        scratch_shapes=[
            pltpu.VMEM((tokens, feats), bf),
            pltpu.VMEM((tokens, feats), bf),
            pltpu.VMEM((cols, feats), bf),
            pltpu.VMEM(outer_params.shape, f32),
            pltpu.VMEM(outer_params.shape, f32),
            pltpu.VMEM(local_params.shape[1:], bf),
            pltpu.VMEM((levels, frows, width), f32),
            pltpu.VMEM((levels, frows, width), f32),
            pltpu.VMEM((2, tokens, width), bf),
            pltpu.VMEM((2, PIECES, n * tp, cols), bf),
            pltpu.VMEM((cols, feats), bf),
            pltpu.VMEM((cols, feats), f32),
            pltpu.VMEM((2, tokens, 128), f32),
            pltpu.VMEM((2, PIECES, 2, half * tp, feats), bf),
            pltpu.VMEM((2, PIECES, half - 1, 2, tp, feats), bf),
            pltpu.VMEM((2, PIECES, tp, feats), f32),
            pltpu.VMEM((2, PIECES, tp, feats), bf),
            pltpu.VMEM((2, PIECES, tp, feats), bf),
            pltpu.VMEM((2, PIECES, n * tp, feats), bf),
            pltpu.SemaphoreType.DMA((2, PIECES + 1)),
            others,
            others,
            peers,
            peers,
            pair,
            pair,
            pair,
            pair,
            peers,
            peers,
            peers,
            peers,
            pltpu.SemaphoreType.DMA((6,)),
            pltpu.SemaphoreType.DMA((levels,)),
            pltpu.SemaphoreType.DMA((levels,)),
        ],
        compiler_params=pltpu.CompilerParams(
            collective_id=0, has_side_effects=True, vmem_limit_bytes=56 * 1024 * 1024
        ),
        cost_estimate=pl.CostEstimate(
            flops=8 * n * tokens * cols * feats,
            bytes_accessed=200 * 1024 * 1024,
            transcendentals=0,
        ),
    )(
        hidden_one,
        hidden_two,
        targets_one,
        targets_two,
        weight,
        fragment,
        outer_params,
        outer_momentum,
        local_params[0],
    )
    return (new_shard[None], errors_two, merged_params, merged_momentum)


def solution(mesh):
    return jax.shard_map(
        per_device,
        mesh=mesh,
        in_specs=(
            P(("replica", "fsdp"), None),
            P(("replica", "fsdp"), None),
            P(("replica", "fsdp"), None),
            P(("replica", "fsdp"), None),
            P("replica", "fsdp", None),
            P(),
            P(None, "fsdp", None),
            P(None, "fsdp", None),
            P("replica", None, "fsdp", None),
        ),
        out_specs=(
            P("replica", "fsdp", None),
            P(("replica", "fsdp"), None),
            P("fsdp", None),
            P("fsdp", None),
        ),
        check_vma=False,
    )
```

```python
import functools

import jax
import jax.numpy as jnp
from jax import lax
from jax.experimental import pallas as pl
from jax.experimental.pallas import tpu as pltpu
from jax.sharding import PartitionSpec as P

EPS = 1e-06
LEARN_RATE = 0.3
OUTER_RATE = 0.7
MOMENTUM = 0.9
MESH = pl.DeviceIdType.MESH
PIECES = 4
WINDOW = 2


def tile_of(extent):
    return 256 if extent % 256 == 0 else 128


def steps_kernel(
    n,
    replicas,
    h_one,
    h_two,
    t_one_hbm,
    t_two_hbm,
    w_hbm,
    fragment,
    params_hbm,
    momentum_hbm,
    local_hbm,
    out_w,
    out_e,
    out_params,
    out_momentum,
    t_one,
    t_two,
    w_ref,
    params,
    momentum,
    local,
    outer_sum,
    outer_in,
    hv,
    xs,
    w_next,
    grad,
    scale,
    vs,
    ra,
    mine,
    rb_out,
    rb_in,
    errs,
    l_sem,
    x_send,
    x_recv,
    a_send,
    a_recv,
    b_send,
    b_recv,
    c_send,
    c_recv,
    i_send,
    i_recv,
    f_send,
    f_recv,
    o_load,
    o_send,
    o_recv,
):
    tokens, width = h_one.shape
    cols, feats = w_ref.shape
    tp = tokens // PIECES
    half = n // 2
    factor = width ** (-0.5)
    me = lax.axis_index("fsdp")
    side, spot = me // half, me % half
    other = 1 - side
    cross = other * half + spot
    hidden = (h_one, h_two)
    targets = (t_one, t_two)

    mine_r = lax.axis_index("replica")
    levels = replicas.bit_length() - 1
    outer_peers = []
    for k in range(levels):
        step = 2**k
        outer_peers.append(mine_r + (1 - 2 * ((mine_r // step) % 2)) * step)

    barrier = pltpu.get_barrier_semaphore()
    for d in range(1, n):
        pl.semaphore_signal(
            barrier, inc=1, device_id={"fsdp": lax.rem(me + d, n)}, device_id_type=MESH
        )
    for peer in outer_peers:
        pl.semaphore_signal(barrier, inc=1, device_id={"replica": peer}, device_id_type=MESH)
    pl.semaphore_wait(barrier, n - 1 + len(outer_peers))

    def remote(src, dst, send, recv, peer):
        return pltpu.make_async_remote_copy(
            src_ref=src,
            dst_ref=dst,
            send_sem=send,
            recv_sem=recv,
            device_id={"fsdp": peer},
            device_id_type=MESH,
        )

    def rows_of(block):
        return pl.ds(pl.multiple_of(block * tp, tp), tp)

    def cols_of(block):
        return pl.ds(pl.multiple_of(block * cols, 128), cols)

    def x_copies(k):
        s, p = k // PIECES, k % PIECES
        out = []
        for d in range(1, n):
            peer = lax.rem(me + d, n)
            out.append(
                remote(
                    hidden[s].at[pl.ds(p * tp, tp), cols_of(peer)],
                    xs.at[s, p, rows_of(me), :],
                    x_send.at[s, p, d - 1],
                    x_recv.at[s, p, d - 1],
                    peer,
                )
            )
        return out

    def half_peers():
        return [(d - 1, side * half + lax.rem(spot + d, half)) for d in range(1, half)]

    def a_copies(s, p):
        return [
            remote(
                vs.at[s, p, :, rows_of(peer - side * half), :],
                ra.at[s, p, d],
                a_send.at[s, p, d],
                a_recv.at[s, p, d],
                peer,
            )
            for d, peer in half_peers()
        ]

    def b_copy(s, p):
        return remote(
            rb_out.at[s, p], rb_in.at[s, p], b_send.at[s, p], b_recv.at[s, p], cross
        )

    def c_copy(s, p):
        piece = errs.at[s, p, rows_of(me), :]
        return remote(piece, piece, c_send.at[s, p], c_recv.at[s, p], cross)

    def i_copies(s, p):
        piece = errs.at[s, p, rows_of(me), :]
        return [
            remote(piece, piece, i_send.at[s, p, d], i_recv.at[s, p, d], peer)
            for d, peer in half_peers()
        ]

    def f_copies(s, p):
        piece = errs.at[s, p, rows_of(cross), :]
        return [
            remote(piece, piece, f_send.at[s, p, d], f_recv.at[s, p, d], peer)
            for d, peer in half_peers()
        ]

    issued = [0]

    def pump():
        k = issued[0]
        if k == 2 * PIECES:
            return
        if k >= WINDOW:
            for copy in x_copies(k - WINDOW):
                copy.wait_send()
        for copy in x_copies(k):
            copy.start()
        issued[0] = k + 1

    for _ in range(WINDOW):
        pump()
    loads = []
    for s in range(2):
        loads.append(pltpu.make_async_copy(hidden[s], hv.at[s], l_sem.at[s, PIECES]))
        for p in range(PIECES):
            loads.append(
                pltpu.make_async_copy(
                    hidden[s].at[pl.ds(p * tp, tp), cols_of(me)],
                    xs.at[s, p, rows_of(me), :],
                    l_sem.at[s, p],
                )
            )
    outer_loads = []
    for i, (src, dst) in enumerate(
        (
            (params_hbm, params),
            (local_hbm, local),
            (momentum_hbm, momentum),
            (w_hbm, w_ref),
            (t_one_hbm, t_one),
            (t_two_hbm, t_two),
        )
    ):
        outer_loads.append(pltpu.make_async_copy(src, dst, o_load.at[i]))
    for copy in outer_loads + loads:
        copy.start()
    for copy in outer_loads:
        copy.wait()
    chosen = lax.rem(fragment[0], params_hbm.shape[0])

    def outer_copy(k):
        return pltpu.make_async_remote_copy(
            src_ref=outer_sum.at[k],
            dst_ref=outer_in.at[k],
            send_sem=o_send.at[k],
            recv_sem=o_recv.at[k],
            device_id={"replica": outer_peers[k]},
            device_id_type=MESH,
        )

    term = params[chosen] - local[chosen].astype(jnp.float32)
    outer_sum[0] = term.astype(jnp.bfloat16).astype(jnp.float32)
    outer_copy(0).start()
    for copy in loads:
        copy.wait()
    for s in range(2):

        @pl.loop(0, tokens // 16)
        def _(i):
            rows = pl.ds(pl.multiple_of(i * 16, 16), 16)
            wide = hv[s, rows, :].astype(jnp.float32)
            mean = jnp.sum(wide * wide, axis=1, keepdims=True) * (1.0 / width)
            scale[s, rows, :] = jnp.broadcast_to(lax.rsqrt(mean + EPS), (16, 128))

    def outer_level(k):
        outer_copy(k).wait_recv()
        total = outer_sum[k] + outer_in[k]
        if k + 1 < levels:
            outer_sum[k + 1] = total
            outer_copy(k + 1).start()
            return
        outer_grad = total * (1.0 / replicas)
        merged = MOMENTUM * momentum[chosen] + outer_grad
        out_momentum[...] = merged
        out_params[...] = params[chosen] - OUTER_RATE * (outer_grad + MOMENTUM * merged)

    outer_done = [0]

    def stage_a(s, p):
        weight = w_ref if s == 0 else w_next
        for copy in x_copies(s * PIECES + p):
            copy.wait_recv()
        nt = tile_of(feats)

        @pl.loop(0, feats // nt)
        def _(j):
            lanes = pl.ds(pl.multiple_of(j * nt, nt), nt)
            part = jnp.dot(xs[s, p], weight[:, lanes], preferred_element_type=jnp.float32)
            vs[s, p, :, :, lanes] = part.astype(jnp.bfloat16).reshape(2, half * tp, nt)

        for copy in a_copies(s, p):
            copy.start()
        pump()

    def stage_b(s, p):
        copies = a_copies(s, p)
        for copy in copies:
            copy.wait_recv()
        spots = rows_of(spot)
        away = vs[s, p, other, spots, :].astype(jnp.float32)
        for d in range(half - 1):
            away = away + ra[s, p, d, other].astype(jnp.float32)
        rb_out[s, p] = away.astype(jnp.bfloat16)
        b_copy(s, p).start()
        here = vs[s, p, side, spots, :].astype(jnp.float32)
        for d in range(half - 1):
            here = here + ra[s, p, d, side].astype(jnp.float32)
        mine[s, p] = here

    def stage_c(s, p):
        b_copy(s, p).wait_recv()
        rows = pl.ds(p * tp, tp)
        gain = scale[s, rows, :][:, :1]
        total = mine[s, p] + rb_in[s, p].astype(jnp.float32)
        err = total * (gain * factor) - targets[s][rows, :].astype(jnp.float32)
        err = err.astype(jnp.bfloat16)
        if s == 1:
            out_e[rows, :] = err
        errs[s, p, rows_of(me), :] = (err.astype(jnp.float32) * gain).astype(jnp.bfloat16)
        c_copy(s, p).start()
        for copy in i_copies(s, p):
            copy.start()

    def stage_d(s, p):
        c_copy(s, p).wait_recv()
        for copy in f_copies(s, p):
            copy.start()

    ct = tile_of(cols)

    def stage_f(s, p):
        for copy in i_copies(s, p) + f_copies(s, p):
            copy.wait_recv()
        source = w_ref if s == 0 else w_next
        target = w_next if s == 0 else out_w

        @pl.loop(0, cols // ct)
        def _(j):
            lanes = pl.ds(pl.multiple_of(j * ct, ct), ct)
            term = lax.dot_general(
                xs[s, p, :, lanes],
                errs[s, p],
                (((0,), (0,)), ((), ())),
                preferred_element_type=jnp.float32,
            )
            if p > 0:
                term = grad[lanes, :] + term
            if p < PIECES - 1:
                grad[lanes, :] = term
            else:
                old = source[lanes, :].astype(jnp.float32)
                target[lanes, :] = (old - (LEARN_RATE * factor) * term).astype(jnp.bfloat16)

    stages = (stage_a, stage_b, stage_c, stage_d, stage_f)
    depth = len(stages)
    for s in range(2):
        for t in range(PIECES + depth - 1):
            for lag in (3, 2, 1, 0, 4):
                if 0 <= t - lag < PIECES:
                    stages[lag](s, t - lag)
            if t >= PIECES:
                pump()
            if outer_done[0] < levels:
                outer_level(outer_done[0])
                outer_done[0] += 1

    for k in range(levels):
        outer_copy(k).wait_send()
    for k in range(2 * PIECES - WINDOW, 2 * PIECES):
        for copy in x_copies(k):
            copy.wait_send()
    for s in range(2):
        for p in range(PIECES):
            for copy in a_copies(s, p) + i_copies(s, p) + f_copies(s, p):
                copy.wait_send()
            b_copy(s, p).wait_send()
            c_copy(s, p).wait_send()


def per_device(
    hidden_one,
    hidden_two,
    targets_one,
    targets_two,
    value_weight,
    fragment,
    outer_params,
    outer_momentum,
    local_params,
):
    weight = value_weight[0]
    n = lax.axis_size("fsdp")
    replicas = lax.axis_size("replica")
    levels = replicas.bit_length() - 1
    frows = outer_params.shape[1]
    half = n // 2
    tokens, width = hidden_one.shape
    cols, feats = weight.shape
    tp = tokens // PIECES
    bf, f32 = jnp.bfloat16, jnp.float32
    anywhere = pl.BlockSpec(memory_space=pl.ANY)
    vmem = pl.BlockSpec(memory_space=pltpu.VMEM)
    pair = pltpu.SemaphoreType.DMA((2, PIECES))
    peers = pltpu.SemaphoreType.DMA((2, PIECES, half - 1))
    others = pltpu.SemaphoreType.DMA((2, PIECES, n - 1))
    new_shard, errors_two, merged_params, merged_momentum = pl.pallas_call(
        functools.partial(steps_kernel, n, replicas),
        out_shape=(
            jax.ShapeDtypeStruct((cols, feats), bf),
            jax.ShapeDtypeStruct((tokens, feats), bf),
            jax.ShapeDtypeStruct((frows, width), f32),
            jax.ShapeDtypeStruct((frows, width), f32),
        ),
        in_specs=[anywhere] * 5 + [pl.BlockSpec(memory_space=pltpu.SMEM)] + [anywhere] * 3,
        out_specs=(vmem, vmem, vmem, vmem),
        scratch_shapes=[
            pltpu.VMEM((tokens, feats), bf),
            pltpu.VMEM((tokens, feats), bf),
            pltpu.VMEM((cols, feats), bf),
            pltpu.VMEM(outer_params.shape, f32),
            pltpu.VMEM(outer_params.shape, f32),
            pltpu.VMEM(local_params.shape[1:], bf),
            pltpu.VMEM((levels, frows, width), f32),
            pltpu.VMEM((levels, frows, width), f32),
            pltpu.VMEM((2, tokens, width), bf),
            pltpu.VMEM((2, PIECES, n * tp, cols), bf),
            pltpu.VMEM((cols, feats), bf),
            pltpu.VMEM((cols, feats), f32),
            pltpu.VMEM((2, tokens, 128), f32),
            pltpu.VMEM((2, PIECES, 2, half * tp, feats), bf),
            pltpu.VMEM((2, PIECES, half - 1, 2, tp, feats), bf),
            pltpu.VMEM((2, PIECES, tp, feats), f32),
            pltpu.VMEM((2, PIECES, tp, feats), bf),
            pltpu.VMEM((2, PIECES, tp, feats), bf),
            pltpu.VMEM((2, PIECES, n * tp, feats), bf),
            pltpu.SemaphoreType.DMA((2, PIECES + 1)),
            others,
            others,
            peers,
            peers,
            pair,
            pair,
            pair,
            pair,
            peers,
            peers,
            peers,
            peers,
            pltpu.SemaphoreType.DMA((6,)),
            pltpu.SemaphoreType.DMA((levels,)),
            pltpu.SemaphoreType.DMA((levels,)),
        ],
        compiler_params=pltpu.CompilerParams(
            collective_id=0, has_side_effects=True, vmem_limit_bytes=56 * 1024 * 1024
        ),
        cost_estimate=pl.CostEstimate(
            flops=8 * n * tokens * cols * feats,
            bytes_accessed=200 * 1024 * 1024,
            transcendentals=0,
        ),
    )(
        hidden_one,
        hidden_two,
        targets_one,
        targets_two,
        weight,
        fragment,
        outer_params,
        outer_momentum,
        local_params[0],
    )
    return (new_shard[None], errors_two, merged_params, merged_momentum)


def solution(mesh):
    return jax.shard_map(
        per_device,
        mesh=mesh,
        in_specs=(
            P(("replica", "fsdp"), None),
            P(("replica", "fsdp"), None),
            P(("replica", "fsdp"), None),
            P(("replica", "fsdp"), None),
            P("replica", "fsdp", None),
            P(),
            P(None, "fsdp", None),
            P(None, "fsdp", None),
            P("replica", None, "fsdp", None),
        ),
        out_specs=(
            P("replica", "fsdp", None),
            P(("replica", "fsdp"), None),
            P("fsdp", None),
            P("fsdp", None),
        ),
        check_vma=False,
    )
```
